32 devices in a mesh: gx: 8 (over y, x, core), gy: 4 (over z).
Axes of the slice: x: 2, y: 2, z: 4, core: 2. Of those that a mesh axis runs over, the one named last changes fastest.
Arguments:
- state: float32 [9, 56, 4096], P(None, None, ('gx', 'gy')), may hold values from -6 to 6
- star_matrices: float32 [3, 9, 9, 4096], P(None, None, None, ('gx', 'gy')), may hold values from -1.25 to 1.25
- stiffness: float32 [3, 56, 56], replicated, may hold values from -0.75 to 0.75
- face_project: float32 [4, 21, 56], replicated, may hold values from -0.75 to 0.75
- flux_inner: float32 [9, 9], replicated, may hold values from -2 to 2
- flux_outer: float32 [9, 9], replicated, may hold values from -2 to 2
- rate_level: int32 [4096], P(('gx', 'gy')), may hold values from 0 to 2
- neighbour: int32 [4, 4096], P(None, ('gx', 'gy')), may hold values from 0 to 511
- send_slots: int32 [4, 8192], P(None, ('gx', 'gy')), may hold values from 0 to 511
- receive_slots: int32 [4, 8192], P(None, ('gx', 'gy')), may hold values from 0 to 511
- fault_faces: int32 [2048], P(('gx', 'gy')), may hold values from 0 to 511, as said below
- slip_flags: int32 [2048], P(('gx', 'gy')), may hold values 0 or 1
Outputs:
- updated: float32 [9, 56, 4096], P(None, None, ('gx', 'gy'))
The draws below stay inside these ranges and needn't reach their ends.
Inputs may be any that keep to these rules, and one draw needn't show every extreme that they name: `neighbour`: local face indices f * 128 + e of the device's own elements. `send_slots`: local face indices of the sending device's own elements. `receive_slots`: local face indices of the receiving device's own elements; two slots may act on one face. `fault_faces`: local face indices of the device's own elements, distinct within one device.
All inputs are finite; a program needn't handle non-finite values. No bound on the sum of `slip_flags` on one device may be relied on, other than what follows from the above.
Results may differ from the reference program's by a relative error of at most 0.0003.
Values sent between devices are 32-bit elements; how exact they have to be, the bound alone decides.
A program may use at most 64 MiB of HBM per device.

```python
import jax
import jax.numpy as jnp
from jax import lax

FIELDS = 9
MODES = 56
FACE_MODES = 21
ORDER = 6
E_DEV = 128
F_NB = 256
FAULT_DEV = 64
ELEMS = 4096
SLOTS = 8192
FAULTS = 2048
N_GX = 8
N_GY = 4


def draw_fault_faces(key, part):
    count = FAULTS // FAULT_DEV
    keys = jax.random.split(jax.random.fold_in(key, 7), count)

    def one_device(single):
        return jax.random.permutation(single, 4 * E_DEV)[:FAULT_DEV].astype(jnp.int32)
    return jax.vmap(one_device)(keys).reshape(FAULTS)


def plant(values, key, least, largest):
    index_at = [jax.random.randint(jax.random.fold_in(key, axis), (), 0, length) for axis, length in enumerate(values.shape)]
    main_axis = values.shape.index(max(values.shape))
    next_to = index_at[:main_axis] + [(index_at[main_axis] + 1) % values.shape[main_axis]] + index_at[main_axis + 1:]
    return values.at[tuple(index_at)].set(least).at[tuple(next_to)].set(largest)


def shard_levels(own_key, dims, shards, smallest, largest):
    def one(position, parts):
        draws = jax.random.uniform(jax.random.fold_in(jax.random.fold_in(own_key, 6), position), (parts,), jnp.float32, smallest / len(shards), largest / len(shards))
        return jnp.repeat(jnp.exp(draws), dims[position] // parts).reshape((-1,) + (1,) * (len(dims) - position - 1))

    factor_of = one(*shards[0])
    for cut in shards[1:]:
        factor_of = factor_of * one(*cut)
    return factor_of


def scatter_about(key, dims, deviation, bound, cuts=(), held_as=jnp.bfloat16):
    gain = shard_levels(key, dims, cuts, -0.22, 0.18) if cuts else 1.0
    result = jax.random.normal(key, dims, jnp.float32) * deviation * gain
    return jnp.minimum(jnp.maximum(result, -bound), bound).astype(held_as)


def setup_inputs(seed: int = 0) -> dict:
    key_of = jax.random.split(jax.random.key(seed), 13)
    return {
        "state": scatter_about(key_of[0], (FIELDS, MODES, ELEMS), 1.0, 6.0, ((2, 32),), jnp.float32),
        "star_matrices": scatter_about(key_of[1], (3, FIELDS, FIELDS, ELEMS), (3 * FIELDS) ** -0.5, 1.25, ((3, 32),), jnp.float32),
        "stiffness": scatter_about(key_of[2], (3, MODES, MODES), MODES ** -0.5, 0.75, (), jnp.float32),
        "face_project": scatter_about(key_of[3], (4, FACE_MODES, MODES), MODES ** -0.5, 0.75, (), jnp.float32),
        "flux_inner": scatter_about(key_of[4], (FIELDS, FIELDS), FIELDS ** -0.5, 2.0, (), jnp.float32),
        "flux_outer": scatter_about(key_of[5], (FIELDS, FIELDS), FIELDS ** -0.5, 2.0, (), jnp.float32),
        "rate_level": plant(jax.random.randint(key_of[6], (ELEMS,), 0, 3), jax.random.fold_in(key_of[6], 1), 0, 2).astype(jnp.int32),
        "neighbour": plant(jax.random.randint(key_of[7], (4, ELEMS), 0, 4 * E_DEV), jax.random.fold_in(key_of[7], 1), 0, (4 * E_DEV) - 1).astype(jnp.int32),
        "send_slots": plant(jax.random.randint(key_of[8], (4, SLOTS), 0, 4 * E_DEV), jax.random.fold_in(key_of[8], 1), 0, (4 * E_DEV) - 1).astype(jnp.int32),
        "receive_slots": plant(jax.random.randint(key_of[9], (4, SLOTS), 0, 4 * E_DEV), jax.random.fold_in(key_of[9], 1), 0, (4 * E_DEV) - 1).astype(jnp.int32),
        "fault_faces": draw_fault_faces(jax.random.fold_in(key_of[12], 71), 0),
        "slip_flags": plant((jax.random.randint(key_of[11], (FAULTS,), 0, 2) < 1).astype(jnp.int32), jax.random.fold_in(key_of[11], 1), 0, 1),
    }


coarse_dt = 2.0
slip_keep = 0.3


def taylor_terms(rate_level):
    step_size = coarse_dt * jnp.exp2(-rate_level.astype(jnp.float32))
    terms = []
    factor = step_size
    for degree in range(ORDER):
        terms.append(factor)
        factor = factor * step_size / (degree + 2.0)
    return terms


def star_apply(star_matrices, modal):
    return jnp.sum(star_matrices[:, :, :, None, :] * modal[:, :, None, :, :], axis=(0, 1))


def derive(current, star_matrices, stiffness):
    modal = jnp.einsum('dmn,qne->dqme', stiffness, current, precision=lax.Precision.HIGHEST)
    return -star_apply(star_matrices, modal)


def volume_term(integral, star_matrices, stiffness):
    modal = jnp.einsum('dnm,qne->dqme', stiffness, integral, precision=lax.Precision.HIGHEST)
    return star_apply(star_matrices, modal)


def on_faces(field, face_project):
    faces = jnp.einsum('fjn,qne->qjfe', face_project, field, precision=lax.Precision.HIGHEST)
    return faces.reshape(FIELDS * FACE_MODES, -1)


def lift_faces(face_terms, face_project):
    shaped = face_terms.reshape(FIELDS, FACE_MODES, 4, -1)
    return jnp.einsum('fjm,qjfe->qme', face_project, shaped, precision=lax.Precision.HIGHEST)


def apply_flux(matrix, face_terms):
    shaped = face_terms.reshape(FIELDS, FACE_MODES, -1)
    mixed = jnp.einsum('qp,qjx->pjx', matrix, shaped, precision=lax.Precision.HIGHEST)
    return mixed.reshape(FIELDS * FACE_MODES, -1)


def keep_mask(fault_faces, slip_flags, count):
    slide = jnp.zeros((4 * count,), jnp.float32).at[fault_faces].set(slip_flags.astype(jnp.float32))
    fields = jnp.arange(FIELDS)
    shear = ((fields >= 3) & (fields < 6)).astype(jnp.float32)
    keep = 1.0 - (1.0 - slip_keep) * shear[:, None] * slide[None, :]
    return jnp.repeat(keep, FACE_MODES, axis=0)


def local_update(state, star_matrices, stiffness, face_project, flux_inner, flux_outer, rate_level, neighbour, send_slots, fault_faces, slip_flags):
    count = state.shape[-1]
    terms = taylor_terms(rate_level)
    current = state
    integral = terms[0] * state
    outer = jnp.zeros((FIELDS * FACE_MODES, 4 * count), jnp.float32)
    flat_neighbour = neighbour.reshape(-1)
    sent = []
    for degree in range(ORDER):
        if degree > 0:
            current = derive(current, star_matrices, stiffness)
            integral = integral + terms[degree] * current
        faces = on_faces(current, face_project)
        outer = outer + jnp.tile(terms[degree], 4)[None, :] * faces[:, flat_neighbour]
        sent.append(faces[:, send_slots])
    inner = on_faces(integral, face_project)
    keep = keep_mask(fault_faces, slip_flags, count)
    flux = apply_flux(flux_inner, inner) + apply_flux(flux_outer, outer * keep)
    fresh = state + volume_term(integral, star_matrices, stiffness) + lift_faces(flux, face_project)
    return fresh, jnp.stack(sent)


def reference(state, star_matrices, stiffness, face_project, flux_inner, flux_outer, rate_level, neighbour, send_slots, receive_slots, fault_faces, slip_flags):
    devices = N_GX * N_GY
    state_dev = jnp.moveaxis(state.reshape(FIELDS, MODES, devices, E_DEV), 2, 0)
    star_dev = jnp.moveaxis(star_matrices.reshape(3, FIELDS, FIELDS, devices, E_DEV), 3, 0)
    level_dev = rate_level.reshape(devices, E_DEV)
    neighbour_dev = jnp.moveaxis(neighbour.reshape(4, devices, E_DEV), 1, 0)
    send_dev = jnp.moveaxis(send_slots.reshape(4, devices, F_NB), 1, 0)
    receive_dev = jnp.moveaxis(receive_slots.reshape(4, devices, F_NB), 1, 0)
    fault_dev = fault_faces.reshape(devices, FAULT_DEV)
    flags_dev = slip_flags.reshape(devices, FAULT_DEV)

    def first(items):
        return local_update(items[0], items[1], stiffness, face_project, flux_inner, flux_outer, items[2], items[3], items[4], items[5], items[6])

    partial_value, stacks = lax.map(first, (state_dev, star_dev, level_dev, neighbour_dev, send_dev, fault_dev, flags_dev))

    def second(items):
        index, level, receive, fault, flags, fresh = items
        column = index // N_GY
        row = index % N_GY
        sources = [index - N_GY, index + N_GY, index - 1, index + 1]
        valid = [column > 0, column < N_GX - 1, row > 0, row < N_GY - 1]
        target_terms = taylor_terms(level[receive % E_DEV])
        count = level.shape[0]
        accum = jnp.zeros((FIELDS * FACE_MODES, 4 * count), jnp.float32)
        for direction in range(4):
            source = jnp.clip(sources[direction], 0, devices - 1)
            stack = lax.dynamic_index_in_dim(stacks, source, 0, keepdims=False)[:, :, direction, :]
            stack = stack * valid[direction].astype(jnp.float32)
            arrived = target_terms[0][direction][None, :] * stack[0]
            for degree in range(1, ORDER):
                arrived = arrived + target_terms[degree][direction][None, :] * stack[degree]
            accum = accum.at[:, receive[direction]].add(arrived)
        keep = keep_mask(fault, flags, count)
        return fresh + lift_faces(apply_flux(flux_outer, accum * keep), face_project)

    indices = jnp.arange(devices, dtype=jnp.int32)
    final = lax.map(second, (indices, level_dev, receive_dev, fault_dev, flags_dev, partial_value))
    return jnp.moveaxis(final, 0, 2).reshape(FIELDS, MODES, devices * E_DEV)
```

```python
import functools

import jax
import jax.numpy as jnp
from jax import lax
from jax.experimental import pallas as pl
from jax.experimental.pallas import tpu as pltpu
from jax.sharding import PartitionSpec as P

ORDER = 6
LEVELS = 3
coarse_dt = 2.0
slip_keep = 0.3
MESH = pl.DeviceIdType.MESH
F32 = jnp.float32
BF16 = jnp.bfloat16


def up(value, unit):
    return -(-value // unit) * unit


def split(value):
    high = value.astype(BF16)
    return high, (value - high.astype(F32)).astype(BF16)


def dot(left, right):
    return jnp.dot(left, right, preferred_element_type=F32)


def dot_nt(left, right):
    return lax.dot_general(left, right, (((1,), (1,)), ((), ())), preferred_element_type=F32)


def one_hot_columns(row, count):
    where = lax.broadcasted_iota(jnp.int32, (count, row.shape[1]), 0)
    return jnp.where(where == row, 1.0, 0.0).astype(BF16)


def triple(weights, pad):
    high, low = split(weights)
    depth = weights.shape[1]
    row = lax.broadcasted_iota(jnp.int32, (depth, 3 * pad), 0)
    column = lax.broadcasted_iota(jnp.int32, (depth, 3 * pad), 1)
    outer_parts = jnp.where((column == row) | (column == row + 2 * pad), 1.0, 0.0).astype(BF16)
    middle = jnp.where(column == row + pad, 1.0, 0.0).astype(BF16)
    return (dot(high, outer_parts) + dot(low, middle)).astype(BF16)


def kernel(
    sizes,
    state, star, stiffness, project, flux_inner, flux_outer, rate, neighbour, send, receive, fault, slip,
    out,
    current, modal, stacked, stacked_level, integral, projected, padded, faces, outer, lifted, base,
    my_level, their_level, outgoing, incoming,
    level_sent, level_got, data_sent, data_got,
):
    gx_count, gy_count = sizes
    fields, modes, count = state.shape
    face_modes = project.shape[1]
    slots = send.shape[1]
    pad = stacked.shape[0] // 3
    face_pad = up(face_modes, 8)
    rows = projected.shape[0] // (2 * LEVELS)
    gx, gy = lax.axis_index("gx"), lax.axis_index("gy")
    below_x, above_x = gx > 0, gx < gx_count - 1
    below_y, above_y = gy > 0, gy < gy_count - 1
    before_x, after_x = (gx - 1, gy), (gx + 1, gy)
    before_y, after_y = (gx, gy - 1), (gx, gy + 1)
    sources = ((below_x, before_x), (above_x, after_x), (below_y, before_y), (above_y, after_y))
    targets = ((above_x, after_x), (below_x, before_x), (above_y, after_y), (below_y, before_y))

    their_level[...] = jnp.zeros_like(their_level)
    incoming[...] = jnp.zeros_like(incoming)
    barrier = pltpu.get_barrier_semaphore()
    for exists, device in sources:
        @pl.when(exists)
        def _():
            pl.semaphore_signal(barrier, inc=1, device_id=device, device_id_type=MESH)
    rate_row = rate[...]
    rate_rows = jnp.broadcast_to(rate_row.astype(F32), (8, count)).astype(BF16)
    for r in range(4):
        element = receive[r : r + 1, :] & (count - 1) if count & (count - 1) == 0 else receive[r : r + 1, :] % count
        my_level[r] = dot(rate_rows, one_hot_columns(element, count))
    expected = sum(exists.astype(jnp.int32) for exists, _ in sources)
    pl.semaphore_wait(barrier, expected)

    def level_copy(r, device):
        return pltpu.make_async_remote_copy(
            src_ref=my_level.at[r], dst_ref=their_level.at[r],
            send_sem=level_sent.at[r], recv_sem=level_got.at[r],
            device_id=device, device_id_type=MESH,
        )

    def data_copy(r, device):
        return pltpu.make_async_remote_copy(
            src_ref=outgoing.at[r], dst_ref=incoming.at[r],
            send_sem=data_sent.at[r], recv_sem=data_got.at[r],
            device_id=device, device_id_type=MESH,
        )

    for r in range(4):
        exists, device = sources[r]

        @pl.when(exists)
        def _():
            level_copy(r, device).start()

    padded[...] = jnp.zeros_like(padded)
    lifted[...] = jnp.zeros_like(lifted)
    projected[...] = jnp.zeros_like(projected)
    faces[...] = jnp.zeros_like(faces)
    for f in range(4):
        padded[f * face_pad : f * face_pad + face_modes, :] = project[f]
    face_weights = padded[...]
    derive_weights = triple(jnp.concatenate([stiffness[d] for d in range(3)], axis=0), pad)
    project_weights = triple(face_weights, pad)

    def stack_parts(target, column, value):
        grown = jnp.concatenate([value, jnp.zeros((pad - modes, count), F32)], axis=0)
        high, low = split(grown)
        at = slice(column, column + count)
        target[0:pad, at] = high
        target[pad : 2 * pad, at] = high
        target[2 * pad : 3 * pad, at] = low

    def star_sum(use):
        for first in range(0, fields, 3):
            group = range(first, min(first + 3, fields))
            totals = [None] * len(group)
            for d in range(3):
                for q in range(fields):
                    part = modal[d * modes : (d + 1) * modes, q * count : (q + 1) * count]
                    for i, p in enumerate(group):
                        term = star[d, q, p : p + 1, :] * part
                        totals[i] = term if totals[i] is None else totals[i] + term
            for i, p in enumerate(group):
                use(p, totals[i])

    steps = [coarse_dt * 0.5**level for level in range(LEVELS)]
    for q in range(fields):
        stack_parts(stacked, q * count, state[q])
        for level in range(LEVELS):
            integral[level, q] = steps[level] * state[q]

    def taylor(degree, factors):
        scale = 1.0 / (degree.astype(F32) + 2.0)
        factors = [factor * (step * scale) for factor, step in zip(factors, steps)]
        modal[0 : 3 * modes, :] = dot(derive_weights, stacked[...])

        def use(p, total):
            value = -total
            stack_parts(stacked, p * count, value)
            for level in range(LEVELS):
                integral[level, p] += factors[level] * value

        star_sum(use)
        return tuple(factors)

    lax.fori_loop(0, ORDER - 1, taylor, tuple(jnp.float32(step) for step in steps))

    width = fields * count
    for level in range(LEVELS):
        for q in range(fields):
            stack_parts(stacked_level, level * width + q * count, integral[level, q])
    for level in range(LEVELS):
        result = dot(project_weights, stacked_level[:, level * width : (level + 1) * width])
        for f in range(4):
            for q in range(fields):
                faces[q * face_modes : (q + 1) * face_modes, f * count : (f + 1) * count] = (
                    result[f * face_pad : f * face_pad + face_modes, q * count : (q + 1) * count]
                )
        high, low = split(faces[...])
        projected[level * rows : (level + 1) * rows, :] = high
        projected[(LEVELS + level) * rows : (LEVELS + level + 1) * rows, :] = low

    def gather(index_row, level_row):
        found = dot(projected[...], one_hot_columns(index_row, 4 * count))
        total = jnp.zeros((rows, index_row.shape[1]), F32)
        for level in range(LEVELS):
            both = found[level * rows : (level + 1) * rows] + found[(LEVELS + level) * rows : (LEVELS + level + 1) * rows]
            total = jnp.where(level_row == level, both, total)
        return total

    for r in (2, 3, 0, 1):
        exists, device = targets[r]

        @pl.when(exists)
        def _():
            level_copy(r, device).wait_recv()
        outgoing[r] = gather(send[r : r + 1, :], their_level[r][0:1, :])

        @pl.when(exists)
        def _():
            data_copy(r, device).start()

    for f in range(4):
        outer[:, f * count : (f + 1) * count] = gather(neighbour[f : f + 1, :], rate_row)

    own = jnp.zeros((1, 1), F32)
    for q in range(fields):
        own = integral[0, q]
        for level in range(1, LEVELS):
            own = jnp.where(rate_row == level, integral[level, q], own)
        stack_parts(stacked, q * count, own)
    own_lift = lax.dot_general(
        face_weights, face_weights, (((0,), (0,)), ((), ())),
        precision=lax.Precision.HIGHEST, preferred_element_type=F32,
    )
    volume_weights = triple(jnp.concatenate([stiffness[d].T for d in range(3)] + [own_lift], axis=0), pad)
    modal[...] = dot(volume_weights, stacked[...])

    def own_flux(p, total):
        total = total + state[p]
        for q in range(fields):
            total = total + flux_inner[q, p] * modal[3 * modes : 4 * modes, q * count : (q + 1) * count]
        base[p] = total

    star_sum(own_flux)

    slide = dot_nt(
        jnp.broadcast_to(slip[...].astype(F32), (8, slip.shape[1])).astype(BF16),
        one_hot_columns(fault[...], 4 * count),
    )[0:1, :]
    slow = 1.0 - (1.0 - slip_keep) * slide

    for r in (0, 1, 2, 3):
        exists, device = sources[r]

        @pl.when(exists)
        def _():
            data_copy(r, device).wait_recv()
        hot = one_hot_columns(receive[r : r + 1, :], 4 * count)
        high, low = split(incoming[r])
        outer[...] += dot_nt(high, hot) + dot_nt(low, hot)

    for q in range(fields):
        for f in range(4):
            part = outer[q * face_modes : (q + 1) * face_modes, f * count : (f + 1) * count]
            if 3 <= q < 6:
                part = part * slow[:, f * count : (f + 1) * count]
            lifted[f * face_pad : f * face_pad + face_modes, q * count : (q + 1) * count] = part
    lift_high, lift_low = split(face_weights.T)
    high, low = split(lifted[...])
    raised = dot(lift_high, high) + dot(lift_low, high) + dot(lift_high, low)
    for p in range(fields):
        total = base[p]
        for q in range(fields):
            total = total + flux_outer[q, p] * raised[:, q * count : (q + 1) * count]
        out[p] = total

    for r in range(4):
        source_exists, source = sources[r]
        target_exists, target = targets[r]

        @pl.when(source_exists)
        def _():
            level_copy(r, source).wait_send()

        @pl.when(target_exists)
        def _():
            data_copy(r, target).wait_send()


def shards(
    sizes,
    state, star_matrices, stiffness, face_project, flux_inner, flux_outer,
    rate_level, neighbour, send_slots, receive_slots, fault_faces, slip_flags,
):
    fields, modes, count = state.shape
    face_modes = face_project.shape[1]
    slots = send_slots.shape[1]
    pad = up(modes, 16)
    face_pad = up(face_modes, 8)
    rows = up(fields * face_modes, 16)
    width = fields * count
    vmem = pl.BlockSpec(memory_space=pltpu.VMEM)
    smem = pl.BlockSpec(memory_space=pltpu.SMEM)
    return pl.pallas_call(
        functools.partial(kernel, sizes),
        out_shape=jax.ShapeDtypeStruct(state.shape, F32),
        in_specs=[vmem] * 4 + [smem] * 2 + [vmem] * 6,
        out_specs=vmem,
        scratch_shapes=[
            pltpu.VMEM((8, 128), F32),
            pltpu.VMEM((4 * modes, width), F32),
            pltpu.VMEM((3 * pad, width), BF16),
            pltpu.VMEM((3 * pad, LEVELS * width), BF16),
            pltpu.VMEM((LEVELS, fields, modes, count), F32),
            pltpu.VMEM((2 * LEVELS * rows, 4 * count), BF16),
            pltpu.VMEM((4 * face_pad, modes), F32),
            pltpu.VMEM((rows, 4 * count), F32),
            pltpu.VMEM((rows, 4 * count), F32),
            pltpu.VMEM((4 * face_pad, width), F32),
            pltpu.VMEM((fields, modes, count), F32),
            pltpu.VMEM((4, 8, slots), F32),
            pltpu.VMEM((4, 8, slots), F32),
            pltpu.VMEM((4, rows, slots), F32),
            pltpu.VMEM((4, rows, slots), F32),
            pltpu.SemaphoreType.DMA((4,)),
            pltpu.SemaphoreType.DMA((4,)),
            pltpu.SemaphoreType.DMA((4,)),
            pltpu.SemaphoreType.DMA((4,)),
        ],
        compiler_params=pltpu.CompilerParams(
            collective_id=0, has_side_effects=True, vmem_limit_bytes=48 * 1024 * 1024
        ),
    )(
        state, star_matrices, stiffness, face_project, flux_inner, flux_outer,
        rate_level.reshape(1, -1), neighbour, send_slots, receive_slots,
        fault_faces.reshape(1, -1), slip_flags.reshape(1, -1),
    )


def solution(mesh):
    both = ("gx", "gy")
    placed = (
        P(None, None, both), P(None, None, None, both), P(), P(), P(), P(),
        P(both), P(None, both), P(None, both), P(None, both), P(both), P(both),
    )
    sizes = (mesh.shape["gx"], mesh.shape["gy"])
    return jax.shard_map(
        functools.partial(shards, sizes), mesh=mesh, in_specs=placed,
        out_specs=P(None, None, both), check_vma=False,
    )
```

```python
import functools

import jax
import jax.numpy as jnp
from jax import lax
from jax.experimental import pallas as pl
from jax.experimental.pallas import tpu as pltpu
from jax.sharding import PartitionSpec as P

ORDER = 6
LEVELS = 3
coarse_dt = 2.0
slip_keep = 0.3
MESH = pl.DeviceIdType.MESH
F32 = jnp.float32
BF16 = jnp.bfloat16


def up(value, unit):
    return -(-value // unit) * unit


def split(value):
    high = value.astype(BF16)
    return high, (value - high.astype(F32)).astype(BF16)


def dot(left, right):
    return jnp.dot(left, right, preferred_element_type=F32)


def dot_nt(left, right):
    return lax.dot_general(left, right, (((1,), (1,)), ((), ())), preferred_element_type=F32)


def one_hot_columns(row, count):
    where = lax.broadcasted_iota(jnp.int32, (count, row.shape[1]), 0)
    return jnp.where(where == row, 1.0, 0.0).astype(BF16)


def triple(weights, pad):
    high, low = split(weights)
    depth = weights.shape[1]
    row = lax.broadcasted_iota(jnp.int32, (depth, 3 * pad), 0)
    column = lax.broadcasted_iota(jnp.int32, (depth, 3 * pad), 1)
    outer_parts = jnp.where((column == row) | (column == row + 2 * pad), 1.0, 0.0).astype(BF16)
    middle = jnp.where(column == row + pad, 1.0, 0.0).astype(BF16)
    return (dot(high, outer_parts) + dot(low, middle)).astype(BF16)


def kernel(
    sizes,
    state_hbm, star_hbm, stiffness_hbm, project_hbm, flux_inner_hbm, flux_outer_hbm, rate_hbm, neighbour_hbm, send_hbm, receive_hbm,
    fault_hbm, slip_hbm,
    out,
    state, star, stiffness, project, flux_inner, flux_outer, rate, neighbour, send, receive, fault, slip, loaded,
    modal, stacked, stacked_level, integral, projected, padded, faces, outer, lifted, base,
    my_level, their_level, outgoing, incoming,
    level_sent, level_got, data_sent, data_got,
):
    gx_count, gy_count = sizes
    given = (receive_hbm, rate_hbm, stiffness_hbm, project_hbm, state_hbm, star_hbm, send_hbm, neighbour_hbm, fault_hbm, slip_hbm,
             flux_inner_hbm, flux_outer_hbm)
    held = (receive, rate, stiffness, project, state, star, send, neighbour, fault, slip, flux_inner, flux_outer)
    loads = [pltpu.make_async_copy(source, target, loaded.at[i]) for i, (source, target) in enumerate(zip(given, held))]
    for load in loads:
        load.start()
    fields, modes, count = state.shape
    face_modes = project.shape[0]
    slots = send.shape[1]
    pad = stacked.shape[0] // 3
    face_pad = up(face_modes, 8)
    rows = projected.shape[0] // (2 * LEVELS)
    gx, gy = lax.axis_index("gx"), lax.axis_index("gy")
    below_x, above_x = gx > 0, gx < gx_count - 1
    below_y, above_y = gy > 0, gy < gy_count - 1
    before_x, after_x = (gx - 1, gy), (gx + 1, gy)
    before_y, after_y = (gx, gy - 1), (gx, gy + 1)
    sources = ((below_x, before_x), (above_x, after_x), (below_y, before_y), (above_y, after_y))
    targets = ((above_x, after_x), (below_x, before_x), (above_y, after_y), (below_y, before_y))

    their_level[...] = jnp.zeros_like(their_level)
    incoming[...] = jnp.zeros_like(incoming)
    barrier = pltpu.get_barrier_semaphore()
    for exists, device in sources:
        @pl.when(exists)
        def _():
            pl.semaphore_signal(barrier, inc=1, device_id=device, device_id_type=MESH)
    loads[0].wait()
    loads[1].wait()
    rate_row = rate[...]
    rate_rows = jnp.broadcast_to(rate_row.astype(F32), (8, count)).astype(BF16)
    for r in range(4):
        element = receive[r : r + 1, :] & (count - 1) if count & (count - 1) == 0 else receive[r : r + 1, :] % count
        my_level[r] = dot(rate_rows, one_hot_columns(element, count))
    padded[...] = jnp.zeros_like(padded)
    lifted[...] = jnp.zeros_like(lifted)
    faces[fields * face_modes - face_modes :, :] = jnp.zeros((rows - (fields - 1) * face_modes, 4 * count), F32)
    loads[2].wait()
    loads[3].wait()
    for f in range(4):
        padded[f * face_pad : f * face_pad + face_modes, :] = project[:, f, :]
    face_weights = padded[...]
    derive_weights = triple(jnp.concatenate([stiffness[d] for d in range(3)], axis=0), pad)
    project_weights = triple(face_weights, pad)
    expected = sum(exists.astype(jnp.int32) for exists, _ in sources)
    pl.semaphore_wait(barrier, expected)

    def level_copy(r, device):
        return pltpu.make_async_remote_copy(
            src_ref=my_level.at[r], dst_ref=their_level.at[r],
            send_sem=level_sent.at[r], recv_sem=level_got.at[r],
            device_id=device, device_id_type=MESH,
        )

    def data_copy(r, device):
        return pltpu.make_async_remote_copy(
            src_ref=outgoing.at[r], dst_ref=incoming.at[r],
            send_sem=data_sent.at[r], recv_sem=data_got.at[r],
            device_id=device, device_id_type=MESH,
        )

    for r in range(4):
        exists, device = sources[r]

        @pl.when(exists)
        def _():
            level_copy(r, device).start()

    for load in loads[4:]:
        load.wait()

    def stack_parts(target, column, value):
        grown = jnp.concatenate([value, jnp.zeros((pad - modes, count), F32)], axis=0)
        high, low = split(grown)
        at = slice(column, column + count)
        target[0:pad, at] = high
        target[pad : 2 * pad, at] = high
        target[2 * pad : 3 * pad, at] = low

    def star_sum(use):
        for first in range(0, fields, 3):
            group = range(first, min(first + 3, fields))
            totals = [None] * len(group)
            for d in range(3):
                for q in range(fields):
                    part = modal[d * modes : (d + 1) * modes, q * count : (q + 1) * count]
                    for i, p in enumerate(group):
                        term = star[q, p, d : d + 1, :] * part
                        totals[i] = term if totals[i] is None else totals[i] + term
            for i, p in enumerate(group):
                use(p, totals[i])

    steps = [coarse_dt * 0.5**level for level in range(LEVELS)]
    for q in range(fields):
        stack_parts(stacked, q * count, state[q])
        for level in range(LEVELS):
            integral[level, q] = steps[level] * state[q]

    def taylor(degree, factors):
        scale = 1.0 / (degree.astype(F32) + 2.0)
        factors = [factor * (step * scale) for factor, step in zip(factors, steps)]
        modal[0 : 3 * modes, :] = dot(derive_weights, stacked[...])

        def use(p, total):
            value = -total
            stack_parts(stacked, p * count, value)
            for level in range(LEVELS):
                integral[level, p] += factors[level] * value

        star_sum(use)
        return tuple(factors)

    lax.fori_loop(0, ORDER - 1, taylor, tuple(jnp.float32(step) for step in steps))

    width = fields * count
    for level in range(LEVELS):
        for q in range(fields):
            stack_parts(stacked_level, level * width + q * count, integral[level, q])
    for level in range(LEVELS):
        result = dot(project_weights, stacked_level[:, level * width : (level + 1) * width])
        for f in range(4):
            for q in range(fields):
                faces[q * face_modes : (q + 1) * face_modes, f * count : (f + 1) * count] = (
                    result[f * face_pad : f * face_pad + face_modes, q * count : (q + 1) * count]
                )
        high, low = split(faces[...])
        projected[level * rows : (level + 1) * rows, :] = high
        projected[(LEVELS + level) * rows : (LEVELS + level + 1) * rows, :] = low

    def gather(index_row, level_row):
        found = dot(projected[...], one_hot_columns(index_row, 4 * count))
        total = jnp.zeros((rows, index_row.shape[1]), F32)
        for level in range(LEVELS):
            both = found[level * rows : (level + 1) * rows] + found[(LEVELS + level) * rows : (LEVELS + level + 1) * rows]
            total = jnp.where(level_row == level, both, total)
        return total

    for pair in ((2, 3), (0, 1)):
        for r in pair:
            exists, device = targets[r]

            @pl.when(exists)
            def _():
                level_copy(r, device).wait_recv()
        index_row = jnp.concatenate([send[r : r + 1, :] for r in pair], axis=1)
        level_row = jnp.concatenate([their_level[r][0:1, :] for r in pair], axis=1)
        found = gather(index_row, level_row)
        for i, r in enumerate(pair):
            outgoing[r] = found[:, i * slots : (i + 1) * slots]
        for r in pair:
            exists, device = targets[r]

            @pl.when(exists)
            def _():
                data_copy(r, device).start()

    outer[...] = gather(
        jnp.concatenate([neighbour[f : f + 1, :] for f in range(4)], axis=1), jnp.concatenate([rate_row] * 4, axis=1)
    )

    own = jnp.zeros((1, 1), F32)
    for q in range(fields):
        own = integral[0, q]
        for level in range(1, LEVELS):
            own = jnp.where(rate_row == level, integral[level, q], own)
        stack_parts(stacked, q * count, own)
    own_lift = lax.dot_general(
        face_weights, face_weights, (((0,), (0,)), ((), ())),
        precision=lax.Precision.HIGHEST, preferred_element_type=F32,
    )
    volume_weights = triple(jnp.concatenate([stiffness[d].T for d in range(3)] + [own_lift], axis=0), pad)
    modal[...] = dot(volume_weights, stacked[...])

    def own_flux(p, total):
        total = total + state[p]
        for q in range(fields):
            total = total + flux_inner[q, p] * modal[3 * modes : 4 * modes, q * count : (q + 1) * count]
        base[p] = total

    star_sum(own_flux)

    slide = dot_nt(
        jnp.broadcast_to(slip[...].astype(F32), (8, slip.shape[1])).astype(BF16),
        one_hot_columns(fault[...], 4 * count),
    )[0:1, :]
    slow = 1.0 - (1.0 - slip_keep) * slide

    for r in (0, 1, 2, 3):
        exists, device = sources[r]

        @pl.when(exists)
        def _():
            data_copy(r, device).wait_recv()
        hot = one_hot_columns(receive[r : r + 1, :], 4 * count)
        high, low = split(incoming[r])
        outer[...] += dot_nt(high, hot) + dot_nt(low, hot)

    for q in range(fields):
        for f in range(4):
            part = outer[q * face_modes : (q + 1) * face_modes, f * count : (f + 1) * count]
            if 3 <= q < 6:
                part = part * slow[:, f * count : (f + 1) * count]
            lifted[f * face_pad : f * face_pad + face_modes, q * count : (q + 1) * count] = part
    lift_high, lift_low = split(face_weights.T)
    high, low = split(lifted[...])
    raised = dot(lift_high, high) + dot(lift_low, high) + dot(lift_high, low)
    for p in range(fields):
        total = base[p]
        for q in range(fields):
            total = total + flux_outer[q, p] * raised[:, q * count : (q + 1) * count]
        out[p] = total

    for r in range(4):
        source_exists, source = sources[r]
        target_exists, target = targets[r]

        @pl.when(source_exists)
        def _():
            level_copy(r, source).wait_send()

        @pl.when(target_exists)
        def _():
            data_copy(r, target).wait_send()


def shards(
    sizes,
    state, star_matrices, stiffness, face_project, flux_inner, flux_outer,
    rate_level, neighbour, send_slots, receive_slots, fault_faces, slip_flags,
):
    fields, modes, count = state.shape
    face_modes = face_project.shape[1]
    slots = send_slots.shape[1]
    pad = up(modes, 16)
    face_pad = up(face_modes, 8)
    rows = up(fields * face_modes, 16)
    width = fields * count
    vmem = pl.BlockSpec(memory_space=pltpu.VMEM)
    hbm = pl.BlockSpec(memory_space=pltpu.HBM)
    given = (
        state, star_matrices.transpose(1, 2, 0, 3), stiffness, face_project.transpose(1, 0, 2), flux_inner, flux_outer,
        rate_level.reshape(1, -1), neighbour, send_slots, receive_slots,
        fault_faces.reshape(1, -1), slip_flags.reshape(1, -1),
    )
    spaces = [pltpu.VMEM] * 4 + [pltpu.SMEM] * 2 + [pltpu.VMEM] * 6
    return pl.pallas_call(
        functools.partial(kernel, sizes),
        out_shape=jax.ShapeDtypeStruct(state.shape, F32),
        in_specs=[hbm] * 12,
        out_specs=vmem,
        scratch_shapes=[space(array.shape, array.dtype) for space, array in zip(spaces, given)] + [
            pltpu.SemaphoreType.DMA((12,)),
            pltpu.VMEM((4 * modes, width), F32),
            pltpu.VMEM((3 * pad, width), BF16),
            pltpu.VMEM((3 * pad, LEVELS * width), BF16),
            pltpu.VMEM((LEVELS, fields, modes, count), F32),
            pltpu.VMEM((2 * LEVELS * rows, 4 * count), BF16),
            pltpu.VMEM((4 * face_pad, modes), F32),
            pltpu.VMEM((rows, 4 * count), F32),
            pltpu.VMEM((rows, 4 * count), F32),
            pltpu.VMEM((4 * face_pad, width), F32),
            pltpu.VMEM((fields, modes, count), F32),
            pltpu.VMEM((4, 8, slots), F32),
            pltpu.VMEM((4, 8, slots), F32),
            pltpu.VMEM((4, rows, slots), F32),
            pltpu.VMEM((4, rows, slots), F32),
            pltpu.SemaphoreType.DMA((4,)),
            pltpu.SemaphoreType.DMA((4,)),
            pltpu.SemaphoreType.DMA((4,)),
            pltpu.SemaphoreType.DMA((4,)),
        ],
        compiler_params=pltpu.CompilerParams(
            collective_id=0, has_side_effects=True, vmem_limit_bytes=64 * 1024 * 1024 - 65536
        ),
    )(*given)


def solution(mesh):
    both = ("gx", "gy")
    placed = (
        P(None, None, both), P(None, None, None, both), P(), P(), P(), P(),
        P(both), P(None, both), P(None, both), P(None, both), P(both), P(both),
    )
    sizes = (mesh.shape["gx"], mesh.shape["gy"])
    return jax.shard_map(
        functools.partial(shards, sizes), mesh=mesh, in_specs=placed,
        out_specs=P(None, None, both), check_vma=False,
    )
```

```python
import functools

import jax
import jax.numpy as jnp
from jax import lax
from jax.experimental import pallas as pl
from jax.experimental.pallas import tpu as pltpu
from jax.sharding import PartitionSpec as P

ORDER = 6
LEVELS = 3
coarse_dt = 2.0
slip_keep = 0.3
MESH = pl.DeviceIdType.MESH
F32 = jnp.float32
BF16 = jnp.bfloat16


def up(value, unit):
    return -(-value // unit) * unit


def split(value):
    high = value.astype(BF16)
    return high, (value - high.astype(F32)).astype(BF16)


def dot(left, right):
    return jnp.dot(left, right, preferred_element_type=F32)


def dot_nt(left, right):
    return lax.dot_general(left, right, (((1,), (1,)), ((), ())), preferred_element_type=F32)


def one_hot_columns(row, count):
    where = lax.broadcasted_iota(jnp.int32, (count, row.shape[1]), 0)
    return jnp.where(where == row, 1.0, 0.0).astype(BF16)


def triple(weights, pad):
    high, low = split(weights)
    depth = weights.shape[1]
    row = lax.broadcasted_iota(jnp.int32, (depth, 3 * pad), 0)
    column = lax.broadcasted_iota(jnp.int32, (depth, 3 * pad), 1)
    outer_parts = jnp.where((column == row) | (column == row + 2 * pad), 1.0, 0.0).astype(BF16)
    middle = jnp.where(column == row + pad, 1.0, 0.0).astype(BF16)
    return (dot(high, outer_parts) + dot(low, middle)).astype(BF16)


def kernel(
    sizes,
    state_hbm, star_hbm, stiffness_hbm, project_hbm, flux_inner_hbm, flux_outer_hbm, rate_hbm, neighbour_hbm, send_hbm, receive_hbm,
    fault_hbm, slip_hbm,
    out,
    state, star, stiffness, project, flux_inner, flux_outer, rate, neighbour, send, receive, fault, slip, loaded,
    modal, stacked, stacked_level, integral, projected, padded, faces, outer, lifted, base,
    my_level, their_level, outgoing, incoming,
    level_sent, level_got, data_sent, data_got,
):
    gx_count, gy_count = sizes
    given = (receive_hbm, rate_hbm, stiffness_hbm, project_hbm, state_hbm, star_hbm, send_hbm, neighbour_hbm, fault_hbm, slip_hbm,
             flux_inner_hbm, flux_outer_hbm)
    held = (receive, rate, stiffness, project, state, star, send, neighbour, fault, slip, flux_inner, flux_outer)
    loads = [pltpu.make_async_copy(source, target, loaded.at[i]) for i, (source, target) in enumerate(zip(given, held))]
    for load in loads:
        load.start()
    fields, modes, count = state.shape
    face_modes = project.shape[0]
    slots = send.shape[1]
    pad = stacked.shape[0] // 3
    face_pad = up(face_modes, 8)
    rows = projected.shape[0] // (2 * LEVELS)
    gx, gy = lax.axis_index("gx"), lax.axis_index("gy")
    below_x, above_x = gx > 0, gx < gx_count - 1
    below_y, above_y = gy > 0, gy < gy_count - 1
    before_x, after_x = (gx - 1, gy), (gx + 1, gy)
    before_y, after_y = (gx, gy - 1), (gx, gy + 1)
    sources = ((below_x, before_x), (above_x, after_x), (below_y, before_y), (above_y, after_y))
    targets = ((above_x, after_x), (below_x, before_x), (above_y, after_y), (below_y, before_y))

    their_level[...] = jnp.zeros_like(their_level)
    incoming[...] = jnp.zeros_like(incoming)
    barrier = pltpu.get_barrier_semaphore()
    for exists, device in sources:
        @pl.when(exists)
        def _():
            pl.semaphore_signal(barrier, inc=1, device_id=device, device_id_type=MESH)
    loads[0].wait()
    loads[1].wait()
    rate_row = rate[...]
    rate_rows = jnp.broadcast_to(rate_row.astype(F32), (8, count)).astype(BF16)
    for r in range(4):
        element = receive[r : r + 1, :] & (count - 1) if count & (count - 1) == 0 else receive[r : r + 1, :] % count
        my_level[r] = dot(rate_rows, one_hot_columns(element, count))
    padded[...] = jnp.zeros_like(padded)
    lifted[...] = jnp.zeros_like(lifted)
    faces[fields * face_modes - face_modes :, :] = jnp.zeros((rows - (fields - 1) * face_modes, 4 * count), F32)
    loads[2].wait()
    loads[3].wait()
    for f in range(4):
        padded[f * face_pad : f * face_pad + face_modes, :] = project[:, f, :]
    face_weights = padded[...]
    derive_weights = triple(jnp.concatenate([stiffness[d] for d in range(3)], axis=0), pad)
    project_weights = triple(face_weights, pad)
    expected = sum(exists.astype(jnp.int32) for exists, _ in sources)
    pl.semaphore_wait(barrier, expected)

    def level_copy(r, device):
        return pltpu.make_async_remote_copy(
            src_ref=my_level.at[r], dst_ref=their_level.at[r],
            send_sem=level_sent.at[r], recv_sem=level_got.at[r],
            device_id=device, device_id_type=MESH,
        )

    def data_copy(r, device):
        return pltpu.make_async_remote_copy(
            src_ref=outgoing.at[r], dst_ref=incoming.at[r],
            send_sem=data_sent.at[r], recv_sem=data_got.at[r],
            device_id=device, device_id_type=MESH,
        )

    for r in range(4):
        exists, device = sources[r]

        @pl.when(exists)
        def _():
            level_copy(r, device).start()

    for load in loads[4:]:
        load.wait()

    def stack_parts(target, column, value):
        grown = jnp.concatenate([value, jnp.zeros((pad - modes, count), F32)], axis=0)
        high, low = split(grown)
        at = slice(column, column + count)
        target[0:pad, at] = high
        target[pad : 2 * pad, at] = high
        target[2 * pad : 3 * pad, at] = low

    def star_sum(use):
        for first in range(0, fields, 3):
            group = range(first, min(first + 3, fields))
            totals = [None] * len(group)
            for d in range(3):
                for q in range(fields):
                    part = modal[d * modes : (d + 1) * modes, q * count : (q + 1) * count]
                    for i, p in enumerate(group):
                        term = star[q, p, d : d + 1, :] * part
                        totals[i] = term if totals[i] is None else totals[i] + term
            for i, p in enumerate(group):
                use(p, totals[i])

    steps = [coarse_dt * 0.5**level for level in range(LEVELS)]
    for q in range(fields):
        stack_parts(stacked, q * count, state[q])
        for level in range(LEVELS):
            integral[level, q] = steps[level] * state[q]

    def taylor(degree, factors):
        scale = 1.0 / (degree.astype(F32) + 2.0)
        factors = [factor * (step * scale) for factor, step in zip(factors, steps)]
        modal[0 : 3 * modes, :] = dot(derive_weights, stacked[...])

        def use(p, total):
            value = -total
            stack_parts(stacked, p * count, value)
            for level in range(LEVELS):
                integral[level, p] += factors[level] * value

        star_sum(use)
        return tuple(factors)

    lax.fori_loop(0, ORDER - 1, taylor, tuple(jnp.float32(step) for step in steps))

    width = fields * count
    for level in range(LEVELS):
        for q in range(fields):
            stack_parts(stacked_level, level * width + q * count, integral[level, q])
    for level in range(LEVELS):
        result = dot(project_weights, stacked_level[:, level * width : (level + 1) * width])
        for f in range(4):
            for q in range(fields):
                faces[q * face_modes : (q + 1) * face_modes, f * count : (f + 1) * count] = (
                    result[f * face_pad : f * face_pad + face_modes, q * count : (q + 1) * count]
                )
        high, low = split(faces[...])
        projected[level * rows : (level + 1) * rows, :] = high
        projected[(LEVELS + level) * rows : (LEVELS + level + 1) * rows, :] = low

    def gather(index_row, level_row):
        found = dot(projected[...], one_hot_columns(index_row, 4 * count))
        total = jnp.zeros((rows, index_row.shape[1]), F32)
        for level in range(LEVELS):
            both = found[level * rows : (level + 1) * rows] + found[(LEVELS + level) * rows : (LEVELS + level + 1) * rows]
            total = jnp.where(level_row == level, both, total)
        return total

    for pair in ((2, 3), (0, 1)):
        for r in pair:
            exists, device = targets[r]

            @pl.when(exists)
            def _():
                level_copy(r, device).wait_recv()
        index_row = jnp.concatenate([send[r : r + 1, :] for r in pair], axis=1)
        level_row = jnp.concatenate([their_level[r][0:1, :] for r in pair], axis=1)
        found = gather(index_row, level_row)
        for i, r in enumerate(pair):
            outgoing[r] = found[:, i * slots : (i + 1) * slots]
        for r in pair:
            exists, device = targets[r]

            @pl.when(exists)
            def _():
                data_copy(r, device).start()

    outer[...] = gather(
        jnp.concatenate([neighbour[f : f + 1, :] for f in range(4)], axis=1), jnp.concatenate([rate_row] * 4, axis=1)
    )

    own = jnp.zeros((1, 1), F32)
    for q in range(fields):
        own = integral[0, q]
        for level in range(1, LEVELS):
            own = jnp.where(rate_row == level, integral[level, q], own)
        stack_parts(stacked, q * count, own)
    own_lift = lax.dot_general(
        face_weights, face_weights, (((0,), (0,)), ((), ())),
        precision=lax.Precision.HIGHEST, preferred_element_type=F32,
    )
    volume_weights = triple(jnp.concatenate([stiffness[d].T for d in range(3)] + [own_lift], axis=0), pad)
    modal[...] = dot(volume_weights, stacked[...])

    def own_flux(p, total):
        total = total + state[p]
        for q in range(fields):
            total = total + flux_inner[q, p] * modal[3 * modes : 4 * modes, q * count : (q + 1) * count]
        base[p] = total

    star_sum(own_flux)

    slide = dot_nt(
        jnp.broadcast_to(slip[...].astype(F32), (8, slip.shape[1])).astype(BF16),
        one_hot_columns(fault[...], 4 * count),
    )[0:1, :]
    slow = 1.0 - (1.0 - slip_keep) * slide

    hots = [one_hot_columns(receive[r : r + 1, :], 4 * count) for r in range(4)]
    lift_high, lift_low = split(face_weights.T)

    for r in (0, 1, 2, 3):
        exists, device = sources[r]

        @pl.when(exists)
        def _():
            data_copy(r, device).wait_recv()
        hot = hots[r]
        high, low = split(incoming[r])
        outer[...] += dot_nt(high, hot) + dot_nt(low, hot)

    for q in range(fields):
        for f in range(4):
            part = outer[q * face_modes : (q + 1) * face_modes, f * count : (f + 1) * count]
            if 3 <= q < 6:
                part = part * slow[:, f * count : (f + 1) * count]
            lifted[f * face_pad : f * face_pad + face_modes, q * count : (q + 1) * count] = part
    high, low = split(lifted[...])
    raised = dot(lift_high, high) + dot(lift_low, high) + dot(lift_high, low)
    for p in range(fields):
        total = base[p]
        for q in range(fields):
            total = total + flux_outer[q, p] * raised[:, q * count : (q + 1) * count]
        out[p] = total

    for r in range(4):
        source_exists, source = sources[r]
        target_exists, target = targets[r]

        @pl.when(source_exists)
        def _():
            level_copy(r, source).wait_send()

        @pl.when(target_exists)
        def _():
            data_copy(r, target).wait_send()


def shards(
    sizes,
    state, star_matrices, stiffness, face_project, flux_inner, flux_outer,
    rate_level, neighbour, send_slots, receive_slots, fault_faces, slip_flags,
):
    fields, modes, count = state.shape
    face_modes = face_project.shape[1]
    slots = send_slots.shape[1]
    pad = up(modes, 16)
    face_pad = up(face_modes, 8)
    rows = up(fields * face_modes, 16)
    width = fields * count
    vmem = pl.BlockSpec(memory_space=pltpu.VMEM)
    hbm = pl.BlockSpec(memory_space=pltpu.HBM)
    given = (
        state, star_matrices.transpose(1, 2, 0, 3), stiffness, face_project.transpose(1, 0, 2), flux_inner, flux_outer,
        rate_level.reshape(1, -1), neighbour, send_slots, receive_slots,
        fault_faces.reshape(1, -1), slip_flags.reshape(1, -1),
    )
    spaces = [pltpu.VMEM] * 4 + [pltpu.SMEM] * 2 + [pltpu.VMEM] * 6
    return pl.pallas_call(
        functools.partial(kernel, sizes),
        out_shape=jax.ShapeDtypeStruct(state.shape, F32),
        in_specs=[hbm] * 12,
        out_specs=vmem,
        scratch_shapes=[space(array.shape, array.dtype) for space, array in zip(spaces, given)] + [
            pltpu.SemaphoreType.DMA((12,)),
            pltpu.VMEM((4 * modes, width), F32),
            pltpu.VMEM((3 * pad, width), BF16),
            pltpu.VMEM((3 * pad, LEVELS * width), BF16),
            pltpu.VMEM((LEVELS, fields, modes, count), F32),
            pltpu.VMEM((2 * LEVELS * rows, 4 * count), BF16),
            pltpu.VMEM((4 * face_pad, modes), F32),
            pltpu.VMEM((rows, 4 * count), F32),
            pltpu.VMEM((rows, 4 * count), F32),
            pltpu.VMEM((4 * face_pad, width), F32),
            pltpu.VMEM((fields, modes, count), F32),
            pltpu.VMEM((4, 8, slots), F32),
            pltpu.VMEM((4, 8, slots), F32),
            pltpu.VMEM((4, rows, slots), F32),
            pltpu.VMEM((4, rows, slots), F32),
            pltpu.SemaphoreType.DMA((4,)),
            pltpu.SemaphoreType.DMA((4,)),
            pltpu.SemaphoreType.DMA((4,)),
            pltpu.SemaphoreType.DMA((4,)),
        ],
        compiler_params=pltpu.CompilerParams(
            collective_id=0, has_side_effects=True, vmem_limit_bytes=64 * 1024 * 1024 - 65536
        ),
    )(*given)


def solution(mesh):
    both = ("gx", "gy")
    placed = (
        P(None, None, both), P(None, None, None, both), P(), P(), P(), P(),
        P(both), P(None, both), P(None, both), P(None, both), P(both), P(both),
    )
    sizes = (mesh.shape["gx"], mesh.shape["gy"])
    return jax.shard_map(
        functools.partial(shards, sizes), mesh=mesh, in_specs=placed,
        out_specs=P(None, None, both), check_vma=False,
    )
```
